32 devices in a mesh: grp: 2 (over x), blk: 16 (over z, y, core).
Axes of the slice: x: 2, y: 2, z: 4, core: 2. Of those that a mesh axis runs over, the one named last changes fastest.
Arguments:
- features: bfloat16 [16384, 256], P(('grp', 'blk')), parts along dimension 0, may hold values from -6 to 6
- tile_rows: int32 [512], P(('grp', 'blk')), parts along dimension 0, may hold values from 0 to 63, as said below
- tile_cols: int32 [512], P(('grp', 'blk')), parts along dimension 0, may hold values from 0 to 63, as said below
- tile_live: int32 [32], P(('grp', 'blk')), parts along dimension 0, may hold values from 4 to 16, as said below
- tile_vals: bfloat16 [512, 128, 128], P(('grp', 'blk')), parts along dimension 0, may hold values from -1 to 1
- w_msg: bfloat16 [3, 256, 256], replicated, may hold values from -0.375 to 0.375
- w_self: bfloat16 [3, 256, 256], replicated, may hold values from -0.375 to 0.375
- w_dec: bfloat16 [256, 128], replicated, may hold values from -0.375 to 0.375
- w_head: float32 [128], replicated, may hold values from -0.5 to 0.5
- sample_pairs: int32 [65536, 2], P(('grp', 'blk')), parts along dimension 0, may hold values from 0 to 8191
- targets: float32 [16384], P(('grp', 'blk')), parts along dimension 0, may hold values from -12 to 12
Outputs:
- objective: float32 [2], P('grp'), parts along dimension 0
- grad_msg: float32 [6, 256, 256], P('grp', 'blk'), parts along dimension 0
- grad_self: float32 [6, 256, 256], P('grp', 'blk'), parts along dimension 0
- grad_dec: float32 [512, 128], P(('grp', 'blk')), parts along dimension 0
- grad_head: float32 [256], P('grp'), parts along dimension 0
- grad_input: float32 [16384, 256], P(('grp', 'blk')), parts along dimension 0
The draws below stay inside these ranges and needn't reach their ends.
There are 2 independent parts, one for each index of `grp`. The reference program is written for one: setup_inputs(seed, part) draws one part's arguments, and reference() takes and returns one part's arrays. A program takes and returns all parts, laid end to end along the dimension named above; an argument that names none is the same for every part. Nothing has to cross between parts.
Inputs may be any that keep to these rules, and one draw needn't show every extreme that they name: `tile_rows`: slot s of device d (slots d * 16 to (d + 1) * 16 - 1) lies in one of that device's row blocks d * 4 to (d + 1) * 4 - 1. `tile_cols`: every slot's column block lies at most 2 blocks from its row block around the cycle of 64 blocks, at that distance in both directions on some slots. `tile_live`: live slots come first on each device; some device has all 16 slots live.
All inputs are finite; a program needn't handle non-finite values.
Results may differ from the reference program's by a relative error of at most 0.015.
Values may be sent and summed in bfloat16 or wider, within the bound.
A program may use at most 64 MiB of HBM per device.

```python
import jax
import jax.numpy as jnp
from jax import lax

H = 256
DEC = 128
LAYERS = 3
TILE = 128
HB = 2
BPD = 4
PAIR_DEV = 2048
TCAP = 16
NODES = 8192
NBLOCKS = 64
TILES = 256
PAIRS = 32768
N_BLK = 16


def row_blocks(key):
    slot_index = jnp.arange(TILES, dtype=jnp.int32)
    owner = slot_index // TCAP
    inside = jax.random.randint(jax.random.fold_in(key, 11), (TILES,), 0, BPD, dtype=jnp.int32)
    return owner * BPD + inside


def draw_tile_rows(key, part):
    return row_blocks(key)


def draw_tile_cols(key, part):
    row_index = row_blocks(key)
    key = jax.random.fold_in(key, 2)
    shift_by = jax.random.randint(key, (TILES,), -HB, HB + 1, dtype=jnp.int32)
    return (row_index + shift_by) % NBLOCKS


def draw_tile_live(key, part):
    key = jax.random.fold_in(key, 3)
    first_key, second_key = jax.random.split(key)
    counts = jax.random.randint(first_key, (N_BLK,), TCAP // 4, TCAP // 2 + 1, dtype=jnp.int32)
    busiest = jax.random.randint(second_key, (), 0, N_BLK, dtype=jnp.int32)
    return jnp.where(jnp.arange(N_BLK, dtype=jnp.int32) == busiest, TCAP, counts).astype(jnp.int32)


def draw_tile_vals(key, part):
    key = jax.random.fold_in(key, 4)
    mask_key, value_key = jax.random.split(key, 2)
    shape = (TILES, TILE, TILE)
    keep = (jax.random.uniform(mask_key, shape) < 0.4).astype(jnp.float32)
    values = jnp.clip(jax.random.normal(value_key, shape) * 0.1, -0.9, 0.9)
    return (keep * values).astype(jnp.bfloat16)


def touch_ends(drawn, key, least, top_value):
    spot = [jax.random.randint(jax.random.fold_in(key, axis), (), 0, length) for axis, length in enumerate(drawn.shape)]
    main_axis = drawn.shape.index(max(drawn.shape))
    beside = spot[:main_axis] + [(spot[main_axis] + 1) % drawn.shape[main_axis]] + spot[main_axis + 1:]
    return drawn.at[tuple(spot)].set(least).at[tuple(beside)].set(top_value)


def level_of(own_key, shape, shards, low, largest):
    def one(axis_at, blocks):
        heights = jax.random.uniform(jax.random.fold_in(jax.random.fold_in(own_key, 6), axis_at), (blocks,), jnp.float32, low / len(shards), largest / len(shards))
        return jnp.repeat(jnp.exp(heights), shape[axis_at] // blocks).reshape((-1,) + (1,) * (len(shape) - axis_at - 1))

    level = one(*shards[0])
    for cut in shards[1:]:
        level = level * one(*cut)
    return level


def bell_draw(stream_key, extent, spread, most, cuts=(), kind=jnp.bfloat16):
    gain = level_of(stream_key, extent, cuts, -0.22, 0.18) if cuts else 1.0
    values = jax.random.normal(stream_key, extent, jnp.float32) * spread * gain
    return jnp.minimum(jnp.maximum(values, -most), most).astype(kind)


def setup_inputs(seed: int = 0, part: int = 0) -> dict:
    streams_of = jax.random.split(jax.random.key(seed), 12)
    part_splits = jax.random.split(jax.random.fold_in(streams_of[11], part), 12)
    features = bell_draw(part_splits[0], (NODES, H), 1.0, 6.0, ((0, 16),))
    tile_rows = draw_tile_rows(jax.random.fold_in(jax.random.fold_in(streams_of[11], part), 71), part)
    tile_cols = draw_tile_cols(jax.random.fold_in(jax.random.fold_in(streams_of[11], part), 71), part)
    tile_live = draw_tile_live(jax.random.fold_in(jax.random.fold_in(streams_of[11], part), 71), part)
    tile_vals = draw_tile_vals(jax.random.fold_in(jax.random.fold_in(streams_of[11], part), 71), part)
    w_msg = bell_draw(streams_of[5], (LAYERS, H, H), H ** -0.5, 0.375)
    w_self = bell_draw(streams_of[6], (LAYERS, H, H), H ** -0.5, 0.375)
    w_dec = bell_draw(streams_of[7], (H, DEC), H ** -0.5, 0.375)
    w_head = bell_draw(streams_of[8], (DEC,), DEC ** -0.5, 0.5, (), jnp.float32)
    sample_pairs = touch_ends(jax.random.randint(part_splits[9], (PAIRS, 2), 0, NODES), jax.random.fold_in(part_splits[9], 1), 0, NODES - 1).astype(jnp.int32)
    targets = bell_draw(part_splits[10], (NODES,), 2.0, 12.0, ((0, 16),), jnp.float32)
    return {"features": features, "tile_rows": tile_rows, "tile_cols": tile_cols, "tile_live": tile_live, "tile_vals": tile_vals, "w_msg": w_msg, "w_self": w_self, "w_dec": w_dec, "w_head": w_head, "sample_pairs": sample_pairs, "targets": targets}


norm_eps = 1e-05

def silu_slope(values):
    squash = jax.nn.sigmoid(values)
    return squash * (1.0 + values * (1.0 - squash))

def live_flags(tile_live):
    slot_index = jnp.arange(TILES, dtype=jnp.int32)
    owner = slot_index // TCAP
    return (slot_index % TCAP < tile_live[owner]).astype(jnp.float32)

def block_product(source, read_index, write_index, tile_vals, flags, transpose):
    blocks = source.reshape(NBLOCKS, TILE, H)

    def visit(total, item):
        read_block, write_block, values, flag = item
        picked = lax.dynamic_index_in_dim(blocks, read_block, 0, keepdims=False)
        if transpose:
            values = values.T
        term = jnp.dot(values, picked, preferred_element_type=jnp.float32) * flag
        current = lax.dynamic_index_in_dim(total, write_block, 0, keepdims=False)
        return (lax.dynamic_update_index_in_dim(total, current + term, write_block, 0), None)
    start = jnp.zeros((NBLOCKS, TILE, H), jnp.float32)
    total, unused = lax.scan(visit, start, (read_index.astype(jnp.int32), write_index.astype(jnp.int32), tile_vals, flags))
    return total.reshape(NODES, H)

def reference(features, tile_rows, tile_cols, tile_live, tile_vals, w_msg, w_self, w_dec, w_head, sample_pairs, targets):
    flags = live_flags(tile_live)
    hidden = features
    saved = []
    summed = jnp.zeros((NODES, H), jnp.float32)
    for layer in range(LAYERS):
        message = block_product(hidden, tile_cols, tile_rows, tile_vals, flags, False).astype(jnp.bfloat16)
        mixed = jnp.dot(message, w_msg[layer], preferred_element_type=jnp.float32) + jnp.dot(hidden, w_self[layer], preferred_element_type=jnp.float32)
        update = hidden.astype(jnp.float32) + jax.nn.silu(mixed)
        inv_rms = lax.rsqrt(lax.optimization_barrier(jnp.mean(update * update, axis=-1, keepdims=True)) + norm_eps)
        saved.append((hidden, message, mixed, update, inv_rms))
        hidden = (update * inv_rms).astype(jnp.bfloat16)
        summed = summed + hidden.astype(jnp.float32)
    pooled = summed.astype(jnp.bfloat16)
    pre_head = jnp.dot(pooled, w_dec, preferred_element_type=jnp.float32)
    activ = jax.nn.silu(pre_head)
    scores = jnp.dot(activ, w_head, precision=lax.Precision.HIGHEST)
    first = sample_pairs[:, 0]
    second = sample_pairs[:, 1]
    margin = scores[first] - scores[second]
    wanted = jax.nn.sigmoid(targets[first] - targets[second])
    objective = jnp.sum(jax.nn.softplus(margin) - wanted * margin) / PAIR_DEV
    d_margin = (jax.nn.sigmoid(margin) - wanted) / PAIR_DEV
    d_scores = jnp.zeros((NODES,), jnp.float32).at[first].add(d_margin).at[second].add(-d_margin)
    d_pre = (d_scores[:, None] * w_head[None, :] * silu_slope(pre_head)).astype(jnp.bfloat16)
    grad_dec = jnp.dot(pooled.T, d_pre, preferred_element_type=jnp.float32)
    grad_head = jnp.dot(activ.T, d_scores, precision=lax.Precision.HIGHEST)
    d_pooled = jnp.dot(d_pre, w_dec.T, preferred_element_type=jnp.float32)
    carried = d_pooled
    msg_grads = [None] * LAYERS
    self_grads = [None] * LAYERS
    for layer in reversed(range(LAYERS)):
        hidden, message, mixed, update, inv_rms = saved[layer]
        cubed = inv_rms * inv_rms * inv_rms
        d_update = inv_rms * carried - update * cubed * lax.optimization_barrier(jnp.mean(carried * update, axis=-1, keepdims=True))
        d_mixed = (d_update * silu_slope(mixed)).astype(jnp.bfloat16)
        msg_grads[layer] = jnp.dot(message.T, d_mixed, preferred_element_type=jnp.float32)
        self_grads[layer] = jnp.dot(hidden.T, d_mixed, preferred_element_type=jnp.float32)
        d_message = jnp.dot(d_mixed, w_msg[layer].T, preferred_element_type=jnp.float32).astype(jnp.bfloat16)
        d_hidden = d_update + jnp.dot(d_mixed, w_self[layer].T, preferred_element_type=jnp.float32)
        d_hidden = d_hidden + block_product(d_message, tile_rows, tile_cols, tile_vals, flags, True)
        if layer > 0:
            carried = d_hidden + d_pooled
        else:
            carried = d_hidden
    return (objective.reshape(1), jnp.stack(msg_grads), jnp.stack(self_grads), grad_dec, grad_head, carried)
```

```python
import functools

import jax
import jax.numpy as jnp
from jax import lax
from jax.experimental import pallas as pl
from jax.experimental.pallas import tpu as pltpu
from jax.sharding import PartitionSpec as P

LAYERS = 3
HB = 2
TABLE_ROWS = 8
PAIR_CHUNK = 512
norm_eps = 1e-05

F32 = jnp.float32
BF16 = jnp.bfloat16


def dot_nn(a, b):
    return jnp.dot(a, b, preferred_element_type=F32)


def dot_nt(a, b):
    return lax.dot_general(a, b, (((1,), (1,)), ((), ())), preferred_element_type=F32)


def dot_tn(a, b):
    return lax.dot_general(a, b, (((0,), (0,)), ((), ())), preferred_element_type=F32)


def two_parts(values):
    upper = values.astype(BF16)
    return upper, (values - upper.astype(F32)).astype(BF16)


def step(
    n,
    tile_rows,
    tile_cols,
    tile_live,
    feat,
    vals,
    w_msg,
    w_self,
    w_dec,
    w_head,
    pairs,
    targets,
    grad_input,
    grad_msg,
    grad_self,
    grad_dec,
    small_out,
    band,
    rim,
    halo,
    hidden,
    message,
    update,
    slope,
    inverse,
    pooled,
    activ,
    head_slope,
    d_pooled,
    carried,
    d_update,
    d_mixed,
    d_message,
    d_halo,
    table,
    d_part,
    d_recv,
    small,
    small_recv,
    dec_part,
    dec_recv,
    w_part,
    w_recv,
    near_send,
    near_recv,
    all_send,
    all_recv,
):
    row_count, width = feat.shape
    slots, tile, _ = vals.shape
    per_device = row_count // tile
    half = HB * tile
    rows_out = width // n
    pair_total = pairs.shape[1]
    block_total = per_device * n
    me = lax.axis_index("blk")
    left, right = lax.rem(me + n - 1, n), lax.rem(me + 1, n)

    def each_peer(act):
        def visit(k, carry):
            act(lax.rem(me + k, n))
            return carry

        lax.fori_loop(1, n, visit, 0)

    barrier = pltpu.get_barrier_semaphore()
    each_peer(
        lambda peer: pl.semaphore_signal(
            barrier, inc=1, device_id={"blk": peer}, device_id_type=pl.DeviceIdType.MESH
        )
    )
    pl.semaphore_wait(barrier, n - 1)

    def near(source, target, kind, side):
        return pltpu.make_async_remote_copy(
            src_ref=source,
            dst_ref=target,
            send_sem=near_send.at[kind, side],
            recv_sem=near_recv.at[kind, 1 - side],
            device_id={"blk": (left, right)[side]},
            device_id_type=pl.DeviceIdType.MESH,
        )

    def near_arrival(target, kind, side):
        return pltpu.make_async_remote_copy(
            src_ref=target,
            dst_ref=target,
            send_sem=near_send.at[kind, side],
            recv_sem=near_recv.at[kind, side],
            device_id={"blk": left},
            device_id_type=pl.DeviceIdType.MESH,
        )

    def far(source, target, kind, peer, slot):
        return pltpu.make_async_remote_copy(
            src_ref=source,
            dst_ref=target,
            send_sem=all_send.at[kind, peer],
            recv_sem=all_recv.at[kind, slot],
            device_id={"blk": peer},
            device_id_type=pl.DeviceIdType.MESH,
        )

    def scatter(parts, received, kind):
        each_peer(lambda peer: far(parts.at[peer], received.at[me], kind, peer, me).start())

    def arrived(received, kind):
        each_peer(lambda peer: far(received.at[peer], received.at[peer], kind, peer, peer).wait_recv())

    def all_sent(part, kind):
        each_peer(lambda peer: far(part, part, kind, peer, me).wait_send())

    halves = (pl.ds(0, half), pl.ds(row_count - half, half))
    middle = pl.ds(half, row_count)
    rim_cols = (pl.ds(0, half), pl.ds(half + row_count, half))
    sent = []

    def send_halves(source, target, kind, side):
        copy = near(source.at[halves[side]], target.at[1 - side], kind, side)
        copy.start()
        sent.append(copy)

    for side in range(2):
        send_halves(feat, halo.at[0], 0, side)

    for r in range(per_device):
        for e in range(HB, per_device + HB):
            if not r <= e <= r + 2 * HB:
                band[pl.ds(r * tile, tile), pl.ds(e * tile, tile)] = jnp.zeros((tile, tile), BF16)
    for r in range(1, HB):
        for e in range(r):
            band[pl.ds(r * tile, tile), pl.ds(e * tile, tile)] = jnp.zeros((tile, tile), BF16)
            far_row, far_col = per_device - 1 - r, per_device + 2 * HB - 1 - e
            band[pl.ds(far_row * tile, tile), pl.ds(far_col * tile, tile)] = jnp.zeros((tile, tile), BF16)
    live = tile_live[0]

    def fill_row(r, carry):
        totals = [jnp.zeros((tile, tile), F32)] * (2 * HB + 1)
        for t in range(slots):
            shift = lax.rem(tile_cols[t] - tile_rows[t] + HB + block_total, block_total)
            here = jnp.logical_and(tile_rows[t] - me * per_device == r, t < live)
            values = vals[t].astype(F32)
            for d in range(2 * HB + 1):
                chosen = jnp.where(jnp.logical_and(here, shift == d), 1.0, 0.0).astype(F32)
                totals[d] = totals[d] + values * chosen
        at_row = pl.ds(pl.multiple_of(r * tile, tile), tile)
        for d in range(2 * HB + 1):
            at_col = pl.ds(pl.multiple_of((r + d) * tile, tile), tile)
            band[at_row, at_col] = totals[d].astype(BF16)
        return carry

    lax.fori_loop(0, per_device, fill_row, 0)
    for side in range(2):
        copy = near(band.at[halves[side], rim_cols[side]], rim.at[1 - side], 6, side)
        copy.start()
        sent.append(copy)

    for layer in range(LAYERS):
        source = feat if layer == 0 else hidden.at[layer - 1]
        centre = dot_nn(band[:, middle], source[...])
        for side in range(2):
            rows = halves[side]
            near_arrival(halo.at[layer, side], layer, side).wait_recv()
            term = dot_nn(band[rows, rim_cols[side]], halo[layer, side])
            here = centre[side * half : (side + 1) * half] + term
            msg = here.astype(BF16)
            message[layer, rows] = msg
            old = source[rows]
            mixed = dot_nn(msg, w_msg[layer]) + dot_nn(old, w_self[layer])
            squash = jax.nn.sigmoid(mixed)
            upd = old.astype(F32) + mixed * squash
            inv = lax.rsqrt(jnp.sum(upd * upd, axis=-1, keepdims=True) * (1.0 / width) + norm_eps)
            hidden[layer, rows] = (upd * inv).astype(BF16)
            if layer + 1 < LAYERS:
                send_halves(hidden.at[layer], halo.at[layer + 1], layer + 1, side)
            update[layer, rows] = upd
            inverse[layer, rows] = inv
            slope[layer, rows] = squash * (1.0 + mixed * (1.0 - squash))

    pool = hidden[0].astype(F32)
    for layer in range(1, LAYERS):
        pool = pool + hidden[layer].astype(F32)
    pooled[...] = pool.astype(BF16)
    pre_head = dot_nn(pooled[...], w_dec[...])
    squash = jax.nn.sigmoid(pre_head)
    act = pre_head * squash
    activ[...] = act
    head_slope[...] = squash * (1.0 + pre_head * (1.0 - squash))
    head_row = w_head[...]
    own_rows = []
    for b in range(per_device):
        block = act[b * tile : (b + 1) * tile] * head_row
        own_rows.append(jnp.sum(jnp.transpose(block), axis=0, keepdims=True))
    own_rows.append(targets[...])
    table[me] = jnp.concatenate(own_rows, axis=0)
    each_peer(lambda peer: far(table.at[me], table.at[me], 0, peer, me).start())
    arrived(table, 0)

    table_rows = n * TABLE_ROWS
    upper, lower = two_parts(table[...].reshape(table_rows, tile))
    chunk = min(PAIR_CHUNK, pair_total)
    total_d = jnp.zeros((table_rows, tile), F32)
    loss = jnp.zeros((1, chunk), F32)
    for c in range(pair_total // chunk):
        span = slice(c * chunk, (c + 1) * chunk)
        index = jnp.concatenate([pairs[0:1, span], pairs[1:2, span]], axis=1)
        lanes = lax.broadcasted_iota(jnp.int32, (tile, 2 * chunk), 0)
        low_hot = jnp.where(lanes == (index & (tile - 1)), 1.0, 0.0).astype(BF16)
        block_id = index >> 7
        place = lax.shift_right_logical(block_id, 2) * TABLE_ROWS + (block_id & 3)
        found = dot_nn(upper, low_hot) + dot_nn(lower, low_hot)
        at_row = lax.broadcasted_iota(jnp.int32, (table_rows, 2 * chunk), 0)
        in_scores = at_row == place
        score = jnp.sum(jnp.where(in_scores, found, 0.0), axis=0, keepdims=True)
        target = jnp.sum(jnp.where(at_row == place + 4, found, 0.0), axis=0, keepdims=True)
        margin = score[:, :chunk] - score[:, chunk:]
        wanted = jax.nn.sigmoid(target[:, :chunk] - target[:, chunk:])
        softplus = jnp.maximum(margin, 0.0) + jnp.log1p(jnp.exp(-jnp.abs(margin)))
        loss = loss + (softplus - wanted * margin)
        d_margin = (jax.nn.sigmoid(margin) - wanted) * (1.0 / pair_total)
        d_both = jnp.concatenate([d_margin, -d_margin], axis=1)
        d_upper = d_both.astype(BF16).astype(F32)
        d_lower = d_both - d_upper
        total_d = total_d + dot_nt(jnp.where(in_scores, d_upper, 0.0).astype(BF16), low_hot)
        total_d = total_d + dot_nt(jnp.where(in_scores, d_lower, 0.0).astype(BF16), low_hot)
    d_part[...] = total_d.reshape(n, TABLE_ROWS, tile)
    scatter(d_part, d_recv, 1)
    d_recv[me] = d_part[me]
    loss_here = jnp.sum(loss, axis=1, keepdims=True) * (1.0 / pair_total)
    arrived(d_recv, 1)
    d_scores = jnp.sum(d_recv[...], axis=0)

    head_sum = jnp.zeros((1, tile), F32)
    for b in range(per_device):
        rows = pl.ds(b * tile, tile)
        column = jnp.transpose(jnp.broadcast_to(d_scores[b : b + 1, :], (tile, tile)))
        head_sum = head_sum + jnp.sum(activ[rows] * column, axis=0, keepdims=True)
        d_pre = (column * head_row * head_slope[rows]).astype(BF16)
        d_mixed[rows, pl.ds(0, tile)] = d_pre
    d_pre = d_mixed[:, pl.ds(0, tile)]
    pooled_grad = dot_nt(d_pre, w_dec[...])
    d_pooled[...] = pooled_grad
    carried[...] = pooled_grad

    def weight_sends(layer):
        msg_term = dot_tn(message[layer], d_mixed[...])
        own = feat[...] if layer == 0 else hidden[layer - 1]
        self_term = dot_tn(own, d_mixed[...])
        for j in range(n):
            cut = slice(j * rows_out, (j + 1) * rows_out)
            w_part[layer, j, 0] = msg_term[cut].astype(w_part.dtype)
            w_part[layer, j, 1] = self_term[cut].astype(w_part.dtype)
        scatter(w_part.at[layer], w_recv.at[layer], 4 + layer)
        w_recv[layer, me] = w_part[layer, me]

    def weight_sums(layer):
        arrived(w_recv.at[layer], 4 + layer)
        total = jnp.sum(w_recv[layer].astype(F32), axis=0)
        grad_msg[layer] = total[0]
        grad_self[layer] = total[1]

    for layer in reversed(range(LAYERS)):
        if layer == LAYERS - 1:
            dec_term = dot_tn(pooled[...], d_pre)
        for side in range(2):
            rows = halves[side]
            inv = inverse[layer, rows]
            upd = update[layer, rows]
            carry = carried[rows]
            along = jnp.sum(carry * upd, axis=-1, keepdims=True) * (1.0 / width)
            d_upd = inv * carry - upd * (inv * inv * inv * along)
            d_update[rows] = d_upd
            mix = (d_upd * slope[layer, rows]).astype(BF16)
            d_mixed[rows] = mix
            d_message[layer, rows] = dot_nt(mix, w_msg[layer]).astype(BF16)
            send_halves(d_message.at[layer], d_halo.at[layer], 3 + layer, side)
        if layer == LAYERS - 1:
            for j in range(n):
                dec_part[j] = dec_term[j * rows_out : (j + 1) * rows_out].astype(dec_part.dtype)
            scatter(dec_part, dec_recv, 2)
            dec_recv[me] = dec_part[me]
            filler = jnp.zeros((TABLE_ROWS - 2, tile), F32)
            loss_row = jnp.broadcast_to(loss_here, (1, tile))
            small[...] = jnp.concatenate([head_sum, loss_row, filler], axis=0)
            each_peer(lambda peer: far(small, small_recv.at[me], 3, peer, me).start())
            small_recv[me] = small[...]
        weight_sends(layer)
        total = d_update[...] + dot_nt(d_mixed[...], w_self[layer])
        total = total + dot_tn(band[:, middle], d_message[layer])
        if layer > 0:
            total = total + d_pooled[...]
        else:
            arrived(dec_recv, 2)
            grad_dec[...] = jnp.sum(dec_recv[...].astype(F32), axis=0)
            arrived(small_recv, 3)
            small_out[...] = jnp.sum(small_recv[...], axis=0)
            weight_sums(2)
        result = carried if layer > 0 else grad_input
        for side in range(2):
            if layer == LAYERS - 1:
                near_arrival(rim.at[side], 6, side).wait_recv()
            near_arrival(d_halo.at[layer, side], 3 + layer, side).wait_recv()
            term = dot_tn(rim[side], d_halo[layer, side])
            result[halves[side]] = total[side * half : (side + 1) * half] + term
    weight_sums(1)
    weight_sums(0)
    for copy in sent:
        copy.wait_send()
    all_sent(table.at[me], 0)
    all_sent(d_part.at[me], 1)
    all_sent(dec_part.at[me], 2)
    all_sent(small, 3)
    for layer in range(LAYERS):
        all_sent(w_part.at[layer, me], 4 + layer)


def shards(
    features,
    tile_rows,
    tile_cols,
    tile_live,
    tile_vals,
    w_msg,
    w_self,
    w_dec,
    w_head,
    sample_pairs,
    targets,
):
    n = lax.axis_size("blk")
    row_count, width = features.shape
    tile = tile_vals.shape[1]
    per_device = row_count // tile
    dec = w_dec.shape[1]
    half = HB * tile
    rows_out = width // n
    wire = BF16 if rows_out % 16 == 0 else F32
    in_smem = pl.BlockSpec(memory_space=pltpu.SMEM)
    in_vmem = pl.BlockSpec(memory_space=pltpu.VMEM)
    outs = pl.pallas_call(
        functools.partial(step, n),
        out_shape=(
            jax.ShapeDtypeStruct((row_count, width), F32),
            jax.ShapeDtypeStruct((LAYERS, rows_out, width), F32),
            jax.ShapeDtypeStruct((LAYERS, rows_out, width), F32),
            jax.ShapeDtypeStruct((rows_out, dec), F32),
            jax.ShapeDtypeStruct((TABLE_ROWS, tile), F32),
        ),
        in_specs=[in_smem] * 3 + [in_vmem] * 8,
        out_specs=(in_vmem,) * 5,
        scratch_shapes=[
            pltpu.VMEM((row_count, row_count + 2 * half), BF16),
            pltpu.VMEM((2, half, half), BF16),
            pltpu.VMEM((LAYERS, 2, half, width), BF16),
            pltpu.VMEM((LAYERS, row_count, width), BF16),
            pltpu.VMEM((LAYERS, row_count, width), BF16),
            pltpu.VMEM((LAYERS, row_count, width), F32),
            pltpu.VMEM((LAYERS, row_count, width), F32),
            pltpu.VMEM((LAYERS, row_count, 1), F32),
            pltpu.VMEM((row_count, width), BF16),
            pltpu.VMEM((row_count, dec), F32),
            pltpu.VMEM((row_count, dec), F32),
            pltpu.VMEM((row_count, width), F32),
            pltpu.VMEM((row_count, width), F32),
            pltpu.VMEM((row_count, width), F32),
            pltpu.VMEM((row_count, width), BF16),
            pltpu.VMEM((LAYERS, row_count, width), BF16),
            pltpu.VMEM((LAYERS, 2, half, width), BF16),
            pltpu.VMEM((n, TABLE_ROWS, tile), F32),
            pltpu.VMEM((n, TABLE_ROWS, tile), F32),
            pltpu.VMEM((n, TABLE_ROWS, tile), F32),
            pltpu.VMEM((TABLE_ROWS, tile), F32),
            pltpu.VMEM((n, TABLE_ROWS, tile), F32),
            pltpu.VMEM((n, rows_out, dec), wire),
            pltpu.VMEM((n, rows_out, dec), wire),
            pltpu.VMEM((LAYERS, n, 2, rows_out, width), wire),
            pltpu.VMEM((LAYERS, n, 2, rows_out, width), wire),
            pltpu.SemaphoreType.DMA((7, 2)),
            pltpu.SemaphoreType.DMA((7, 2)),
            pltpu.SemaphoreType.DMA((7, n)),
            pltpu.SemaphoreType.DMA((7, n)),
        ],
        compiler_params=pltpu.CompilerParams(
            collective_id=0, has_side_effects=True, vmem_limit_bytes=56 * 1024 * 1024
        ),
        name="ranker_step",
    )(
        tile_rows,
        tile_cols,
        tile_live,
        features,
        tile_vals,
        w_msg,
        w_self,
        w_dec,
        w_head.reshape(1, dec),
        sample_pairs.T,
        targets.reshape(per_device, tile),
    )
    grad_input, grad_msg, grad_self, grad_dec, small = outs
    return small[1, :1], grad_msg, grad_self, grad_dec, small[0], grad_input


def solution(mesh):
    in_specs = (
        P(("grp", "blk"), None),
        P(("grp", "blk")),
        P(("grp", "blk")),
        P(("grp", "blk")),
        P(("grp", "blk"), None, None),
        P(),
        P(),
        P(),
        P(),
        P(("grp", "blk"), None),
        P(("grp", "blk")),
    )
    out_specs = (
        P("grp"),
        P("grp", "blk", None),
        P("grp", "blk", None),
        P(("grp", "blk"), None),
        P("grp"),
        P(("grp", "blk"), None),
    )
    return jax.shard_map(shards, mesh=mesh, in_specs=in_specs, out_specs=out_specs, check_vma=False)
```

```python
import functools

import jax
import jax.numpy as jnp
from jax import lax
from jax.experimental import pallas as pl
from jax.experimental.pallas import tpu as pltpu
from jax.sharding import PartitionSpec as P

LAYERS = 3
HB = 2
TABLE_ROWS = 8
PAIR_CHUNK = 512
norm_eps = 1e-05

F32 = jnp.float32
BF16 = jnp.bfloat16


def dot_nn(a, b):
    return jnp.dot(a, b, preferred_element_type=F32)


def dot_nt(a, b):
    return lax.dot_general(a, b, (((1,), (1,)), ((), ())), preferred_element_type=F32)


def dot_tn(a, b):
    return lax.dot_general(a, b, (((0,), (0,)), ((), ())), preferred_element_type=F32)


def two_parts(values):
    upper = values.astype(BF16)
    return upper, (values - upper.astype(F32)).astype(BF16)


def step(
    n,
    tile_rows,
    tile_cols,
    tile_live,
    feat,
    vals_in,
    w_msg_in,
    w_self_in,
    w_dec_in,
    w_head,
    pairs,
    targets,
    grad_input,
    grad_msg,
    grad_self,
    grad_dec,
    small_out,
    vals,
    w_msg,
    w_self,
    w_dec,
    band,
    rim,
    halo,
    hidden,
    message,
    update,
    slope,
    inverse,
    pooled,
    activ,
    head_slope,
    d_pooled,
    carried,
    d_update,
    d_mixed,
    d_message,
    d_halo,
    table,
    d_part,
    d_recv,
    small,
    small_recv,
    dec_part,
    dec_recv,
    w_part,
    w_near,
    w_sum,
    w_recv,
    target_table,
    load_sem,
    pair_send,
    pair_recv,
    chip_send,
    chip_recv,
    near_send,
    near_recv,
    all_send,
    all_recv,
):
    row_count, width = feat.shape
    slots, tile, _ = vals.shape
    per_device = row_count // tile
    half = HB * tile
    rows_out = width // n
    pair_total = pairs.shape[1]
    block_total = per_device * n
    me = lax.axis_index("blk")
    left, right = lax.rem(me + n - 1, n), lax.rem(me + 1, n)

    def each_peer(act):
        def visit(k, carry):
            act(lax.rem(me + k, n))
            return carry

        lax.fori_loop(1, n, visit, 0)

    loads = [
        pltpu.make_async_copy(there, here, load_sem.at[i])
        for i, (there, here) in enumerate(
            ((vals_in, vals), (w_msg_in, w_msg), (w_self_in, w_self), (w_dec_in, w_dec))
        )
    ]
    for load in loads:
        load.start()
    filler = jnp.zeros((TABLE_ROWS - per_device, tile), F32)
    target_table[me] = jnp.concatenate([targets[...], filler], axis=0)
    barrier = pltpu.get_barrier_semaphore()
    each_peer(
        lambda peer: pl.semaphore_signal(
            barrier, inc=1, device_id={"blk": peer}, device_id_type=pl.DeviceIdType.MESH
        )
    )
    pl.semaphore_wait(barrier, n - 1)

    def near(source, target, kind, side):
        return pltpu.make_async_remote_copy(
            src_ref=source,
            dst_ref=target,
            send_sem=near_send.at[kind, side],
            recv_sem=near_recv.at[kind, 1 - side],
            device_id={"blk": (left, right)[side]},
            device_id_type=pl.DeviceIdType.MESH,
        )

    def near_arrival(target, kind, side):
        return pltpu.make_async_remote_copy(
            src_ref=target,
            dst_ref=target,
            send_sem=near_send.at[kind, side],
            recv_sem=near_recv.at[kind, side],
            device_id={"blk": left},
            device_id_type=pl.DeviceIdType.MESH,
        )

    def far(source, target, kind, peer, slot):
        return pltpu.make_async_remote_copy(
            src_ref=source,
            dst_ref=target,
            send_sem=all_send.at[kind, peer],
            recv_sem=all_recv.at[kind, slot],
            device_id={"blk": peer},
            device_id_type=pl.DeviceIdType.MESH,
        )

    def scatter(parts, received, kind):
        each_peer(lambda peer: far(parts.at[peer], received.at[me], kind, peer, me).start())

    def arrived(received, kind):
        each_peer(lambda peer: far(received.at[peer], received.at[peer], kind, peer, peer).wait_recv())

    def all_sent(part, kind):
        each_peer(lambda peer: far(part, part, kind, peer, me).wait_send())

    halves = (pl.ds(0, half), pl.ds(row_count - half, half))
    middle = pl.ds(half, row_count)
    rim_cols = (pl.ds(0, half), pl.ds(half + row_count, half))
    sent = []

    def send_halves(source, target, kind, side):
        copy = near(source.at[halves[side]], target.at[1 - side], kind, side)
        copy.start()
        sent.append(copy)

    for side in range(2):
        send_halves(feat, halo.at[0], 0, side)

    each_peer(lambda peer: far(target_table.at[me], target_table.at[me], 4, peer, me).start())
    loads[0].wait()

    for r in range(per_device):
        for e in range(HB, per_device + HB):
            if not r <= e <= r + 2 * HB:
                band[pl.ds(r * tile, tile), pl.ds(e * tile, tile)] = jnp.zeros((tile, tile), BF16)
    for r in range(1, HB):
        for e in range(r):
            band[pl.ds(r * tile, tile), pl.ds(e * tile, tile)] = jnp.zeros((tile, tile), BF16)
            far_row, far_col = per_device - 1 - r, per_device + 2 * HB - 1 - e
            band[pl.ds(far_row * tile, tile), pl.ds(far_col * tile, tile)] = jnp.zeros((tile, tile), BF16)
    live = tile_live[0]

    def fill_row(r, carry):
        totals = [jnp.zeros((tile, tile), F32)] * (2 * HB + 1)
        for t in range(slots):
            shift = lax.rem(tile_cols[t] - tile_rows[t] + HB + block_total, block_total)
            here = jnp.logical_and(tile_rows[t] - me * per_device == r, t < live)
            values = vals[t].astype(F32)
            for d in range(2 * HB + 1):
                chosen = jnp.where(jnp.logical_and(here, shift == d), 1.0, 0.0).astype(F32)
                totals[d] = totals[d] + values * chosen
        at_row = pl.ds(pl.multiple_of(r * tile, tile), tile)
        for d in range(2 * HB + 1):
            at_col = pl.ds(pl.multiple_of((r + d) * tile, tile), tile)
            band[at_row, at_col] = totals[d].astype(BF16)
        return carry

    lax.fori_loop(0, per_device, fill_row, 0)
    for side in range(2):
        copy = near(band.at[halves[side], rim_cols[side]], rim.at[1 - side], 6, side)
        copy.start()
        sent.append(copy)

    for load in loads[1:]:
        load.wait()
    for layer in range(LAYERS):
        source = feat if layer == 0 else hidden.at[layer - 1]
        centre = dot_nn(band[:, middle], source[...])
        for side in range(2):
            rows = halves[side]
            near_arrival(halo.at[layer, side], layer, side).wait_recv()
            term = dot_nn(band[rows, rim_cols[side]], halo[layer, side])
            here = centre[side * half : (side + 1) * half] + term
            msg = here.astype(BF16)
            message[layer, rows] = msg
            old = source[rows]
            mixed = dot_nn(msg, w_msg[layer]) + dot_nn(old, w_self[layer])
            squash = jax.nn.sigmoid(mixed)
            upd = old.astype(F32) + mixed * squash
            inv = lax.rsqrt(jnp.sum(upd * upd, axis=-1, keepdims=True) * (1.0 / width) + norm_eps)
            hidden[layer, rows] = (upd * inv).astype(BF16)
            if layer + 1 < LAYERS:
                send_halves(hidden.at[layer], halo.at[layer + 1], layer + 1, side)
            update[layer, rows] = upd
            inverse[layer, rows] = inv
            slope[layer, rows] = squash * (1.0 + mixed * (1.0 - squash))

    pool = hidden[0].astype(F32)
    for layer in range(1, LAYERS):
        pool = pool + hidden[layer].astype(F32)
    pooled[...] = pool.astype(BF16)
    pre_head = dot_nn(pooled[...], w_dec[...])
    squash = jax.nn.sigmoid(pre_head)
    act = pre_head * squash
    activ[...] = act
    head_slope[...] = squash * (1.0 + pre_head * (1.0 - squash))
    head_row = w_head[...]
    own_rows = []
    for b in range(per_device):
        block = act[b * tile : (b + 1) * tile] * head_row
        own_rows.append(jnp.sum(jnp.transpose(block), axis=0, keepdims=True))
    own_rows.append(filler)
    table[me] = jnp.concatenate(own_rows, axis=0)
    each_peer(lambda peer: far(table.at[me], table.at[me], 0, peer, me).start())

    arrived(target_table, 4)
    table_rows = n * TABLE_ROWS
    chunk = min(PAIR_CHUNK, pair_total)
    upper, lower = two_parts(target_table[...].reshape(table_rows, tile))
    lanes = lax.broadcasted_iota(jnp.int32, (tile, 2 * chunk), 0)
    at_row = lax.broadcasted_iota(jnp.int32, (table_rows, 2 * chunk), 0)
    prepared = []
    for c in range(pair_total // chunk):
        span = slice(c * chunk, (c + 1) * chunk)
        index = jnp.concatenate([pairs[0:1, span], pairs[1:2, span]], axis=1)
        low_hot = jnp.where(lanes == (index & (tile - 1)), 1.0, 0.0).astype(BF16)
        block_id = index >> 7
        place = lax.shift_right_logical(block_id, 2) * TABLE_ROWS + (block_id & 3)
        found = dot_nn(upper, low_hot) + dot_nn(lower, low_hot)
        target = jnp.sum(jnp.where(at_row == place, found, 0.0), axis=0, keepdims=True)
        wanted = jax.nn.sigmoid(target[:, :chunk] - target[:, chunk:])
        prepared.append((low_hot, place, wanted))
    arrived(table, 0)

    upper, lower = two_parts(table[...].reshape(table_rows, tile))
    total_d = jnp.zeros((table_rows, tile), F32)
    loss = jnp.zeros((1, chunk), F32)
    for low_hot, place, wanted in prepared:
        found = dot_nn(upper, low_hot) + dot_nn(lower, low_hot)
        in_scores = at_row == place
        score = jnp.sum(jnp.where(in_scores, found, 0.0), axis=0, keepdims=True)
        margin = score[:, :chunk] - score[:, chunk:]
        softplus = jnp.maximum(margin, 0.0) + jnp.log1p(jnp.exp(-jnp.abs(margin)))
        loss = loss + (softplus - wanted * margin)
        d_margin = (jax.nn.sigmoid(margin) - wanted) * (1.0 / pair_total)
        d_both = jnp.concatenate([d_margin, -d_margin], axis=1)
        d_upper = d_both.astype(BF16).astype(F32)
        d_lower = d_both - d_upper
        total_d = total_d + dot_nt(jnp.where(in_scores, d_upper, 0.0).astype(BF16), low_hot)
        total_d = total_d + dot_nt(jnp.where(in_scores, d_lower, 0.0).astype(BF16), low_hot)
    d_part[...] = total_d.reshape(n, TABLE_ROWS, tile)
    scatter(d_part, d_recv, 1)
    d_recv[me] = d_part[me]
    loss_here = jnp.sum(loss, axis=1, keepdims=True) * (1.0 / pair_total)
    arrived(d_recv, 1)
    d_scores = jnp.sum(d_recv[...], axis=0)

    head_sum = jnp.zeros((1, tile), F32)
    for b in range(per_device):
        rows = pl.ds(b * tile, tile)
        column = jnp.transpose(jnp.broadcast_to(d_scores[b : b + 1, :], (tile, tile)))
        head_sum = head_sum + jnp.sum(activ[rows] * column, axis=0, keepdims=True)
        d_pre = (column * head_row * head_slope[rows]).astype(BF16)
        d_mixed[rows, pl.ds(0, tile)] = d_pre
    d_pre = d_mixed[:, pl.ds(0, tile)]
    pooled_grad = dot_nt(d_pre, w_dec[...])
    d_pooled[...] = pooled_grad
    carried[...] = pooled_grad

    def weight_sends(layer):
        msg_term = dot_tn(message[layer], d_mixed[...])
        own = feat[...] if layer == 0 else hidden[layer - 1]
        self_term = dot_tn(own, d_mixed[...])
        for j in range(n):
            cut = slice(j * rows_out, (j + 1) * rows_out)
            w_part[layer, j % 2, j // 2, 0] = msg_term[cut].astype(w_part.dtype)
            w_part[layer, j % 2, j // 2, 1] = self_term[cut].astype(w_part.dtype)
        beside(layer).start()

    core, chip, chips = lax.rem(me, 2), me // 2, n // 2

    def beside(layer):
        return pltpu.make_async_remote_copy(
            src_ref=w_part.at[layer, 1 - core],
            dst_ref=w_near.at[layer],
            send_sem=pair_send.at[layer],
            recv_sem=pair_recv.at[layer],
            device_id={"blk": me + 1 - 2 * core},
            device_id_type=pl.DeviceIdType.MESH,
        )

    def chip_copy(layer, other, slot):
        return pltpu.make_async_remote_copy(
            src_ref=w_sum.at[layer, other],
            dst_ref=w_recv.at[layer, slot],
            send_sem=chip_send.at[layer, other],
            recv_sem=chip_recv.at[layer, slot],
            device_id={"blk": other * 2 + core},
            device_id_type=pl.DeviceIdType.MESH,
        )

    def each_chip(act):
        def visit(k, carry):
            act(lax.rem(chip + k, chips))
            return carry

        lax.fori_loop(1, chips, visit, 0)

    def chip_sends(layer):
        beside(layer).wait_recv()
        both = w_part[layer, core].astype(F32) + w_near[layer].astype(F32)
        w_sum[layer] = both.astype(w_sum.dtype)
        each_chip(lambda other: chip_copy(layer, other, chip).start())
        w_recv[layer, chip] = w_sum[layer, chip]

    def weight_sums(layer):
        each_chip(lambda other: chip_copy(layer, other, other).wait_recv())
        total = jnp.sum(w_recv[layer].astype(F32), axis=0)
        grad_msg[layer] = total[0]
        grad_self[layer] = total[1]

    for layer in reversed(range(LAYERS)):
        if layer == LAYERS - 1:
            dec_term = dot_tn(pooled[...], d_pre)
        for side in range(2):
            rows = halves[side]
            inv = inverse[layer, rows]
            upd = update[layer, rows]
            carry = carried[rows]
            along = jnp.sum(carry * upd, axis=-1, keepdims=True) * (1.0 / width)
            d_upd = inv * carry - upd * (inv * inv * inv * along)
            d_update[rows] = d_upd
            mix = (d_upd * slope[layer, rows]).astype(BF16)
            d_mixed[rows] = mix
            d_message[layer, rows] = dot_nt(mix, w_msg[layer]).astype(BF16)
            send_halves(d_message.at[layer], d_halo.at[layer], 3 + layer, side)
        if layer == LAYERS - 1:
            for j in range(n):
                dec_part[j] = dec_term[j * rows_out : (j + 1) * rows_out].astype(dec_part.dtype)
            scatter(dec_part, dec_recv, 2)
            dec_recv[me] = dec_part[me]
            below = jnp.zeros((TABLE_ROWS - 2, tile), F32)
            loss_row = jnp.broadcast_to(loss_here, (1, tile))
            small[...] = jnp.concatenate([head_sum, loss_row, below], axis=0)
            each_peer(lambda peer: far(small, small_recv.at[me], 3, peer, me).start())
            small_recv[me] = small[...]
        weight_sends(layer)
        total = d_update[...] + dot_nt(d_mixed[...], w_self[layer])
        total = total + dot_tn(band[:, middle], d_message[layer])
        chip_sends(layer)
        if layer > 0:
            total = total + d_pooled[...]
        else:
            arrived(dec_recv, 2)
            grad_dec[...] = jnp.sum(dec_recv[...].astype(F32), axis=0)
            arrived(small_recv, 3)
            small_out[...] = jnp.sum(small_recv[...], axis=0)
            weight_sums(2)
        result = carried if layer > 0 else grad_input
        for side in range(2):
            if layer == LAYERS - 1:
                near_arrival(rim.at[side], 6, side).wait_recv()
            near_arrival(d_halo.at[layer, side], 3 + layer, side).wait_recv()
            term = dot_tn(rim[side], d_halo[layer, side])
            result[halves[side]] = total[side * half : (side + 1) * half] + term
    weight_sums(1)
    weight_sums(0)
    for copy in sent:
        copy.wait_send()
    all_sent(table.at[me], 0)
    all_sent(d_part.at[me], 1)
    all_sent(dec_part.at[me], 2)
    all_sent(small, 3)
    all_sent(target_table.at[me], 4)
    for layer in range(LAYERS):
        beside(layer).wait_send()
        each_chip(lambda other: chip_copy(layer, other, chip).wait_send())


def hand_out(*refs):
    for source, target in zip(refs[:4], refs[5:9]):
        target[...] = source[...]
    small, grad_head, objective = refs[4], refs[9], refs[10]
    grad_head[...] = small[0:1]
    objective[...] = small[1:2, 0:1]


def shards(
    features,
    tile_rows,
    tile_cols,
    tile_live,
    tile_vals,
    w_msg,
    w_self,
    w_dec,
    w_head,
    sample_pairs,
    targets,
):
    n = lax.axis_size("blk")
    row_count, width = features.shape
    tile = tile_vals.shape[1]
    per_device = row_count // tile
    dec = w_dec.shape[1]
    half = HB * tile
    rows_out = width // n
    wire = BF16 if rows_out % 16 == 0 else F32
    in_smem = pl.BlockSpec(memory_space=pltpu.SMEM)
    in_vmem = pl.BlockSpec(memory_space=pltpu.VMEM)
    outs = pl.pallas_call(
        functools.partial(step, n),
        out_shape=(
            jax.ShapeDtypeStruct((row_count, width), F32),
            jax.ShapeDtypeStruct((LAYERS, rows_out, width), F32),
            jax.ShapeDtypeStruct((LAYERS, rows_out, width), F32),
            jax.ShapeDtypeStruct((rows_out, dec), F32),
            jax.ShapeDtypeStruct((TABLE_ROWS, tile), F32),
        ),
        in_specs=[in_smem] * 3 + [in_vmem] + [pl.BlockSpec(memory_space=pl.ANY)] * 4 + [in_vmem] * 3,
        out_specs=(in_vmem,) * 5,
        scratch_shapes=[
            pltpu.VMEM(tile_vals.shape, BF16),
            pltpu.VMEM(w_msg.shape, BF16),
            pltpu.VMEM(w_self.shape, BF16),
            pltpu.VMEM(w_dec.shape, BF16),
            pltpu.VMEM((row_count, row_count + 2 * half), BF16),
            pltpu.VMEM((2, half, half), BF16),
            pltpu.VMEM((LAYERS, 2, half, width), BF16),
            pltpu.VMEM((LAYERS, row_count, width), BF16),
            pltpu.VMEM((LAYERS, row_count, width), BF16),
            pltpu.VMEM((LAYERS, row_count, width), F32),
            pltpu.VMEM((LAYERS, row_count, width), F32),
            pltpu.VMEM((LAYERS, row_count, 1), F32),
            pltpu.VMEM((row_count, width), BF16),
            pltpu.VMEM((row_count, dec), F32),
            pltpu.VMEM((row_count, dec), F32),
            pltpu.VMEM((row_count, width), F32),
            pltpu.VMEM((row_count, width), F32),
            pltpu.VMEM((row_count, width), F32),
            pltpu.VMEM((row_count, width), BF16),
            pltpu.VMEM((LAYERS, row_count, width), BF16),
            pltpu.VMEM((LAYERS, 2, half, width), BF16),
            pltpu.VMEM((n, TABLE_ROWS, tile), F32),
            pltpu.VMEM((n, TABLE_ROWS, tile), F32),
            pltpu.VMEM((n, TABLE_ROWS, tile), F32),
            pltpu.VMEM((TABLE_ROWS, tile), F32),
            pltpu.VMEM((n, TABLE_ROWS, tile), F32),
            pltpu.VMEM((n, rows_out, dec), wire),
            pltpu.VMEM((n, rows_out, dec), wire),
            pltpu.VMEM((LAYERS, 2, n // 2, 2, rows_out, width), wire),
            pltpu.VMEM((LAYERS, n // 2, 2, rows_out, width), wire),
            pltpu.VMEM((LAYERS, n // 2, 2, rows_out, width), wire),
            pltpu.VMEM((LAYERS, n // 2, 2, rows_out, width), wire),
            pltpu.VMEM((n, TABLE_ROWS, tile), F32),
            pltpu.SemaphoreType.DMA((4,)),
            pltpu.SemaphoreType.DMA((LAYERS,)),
            pltpu.SemaphoreType.DMA((LAYERS,)),
            pltpu.SemaphoreType.DMA((LAYERS, n // 2)),
            pltpu.SemaphoreType.DMA((LAYERS, n // 2)),
            pltpu.SemaphoreType.DMA((7, 2)),
            pltpu.SemaphoreType.DMA((7, 2)),
            pltpu.SemaphoreType.DMA((5, n)),
            pltpu.SemaphoreType.DMA((5, n)),
        ],
        compiler_params=pltpu.CompilerParams(
            collective_id=0, has_side_effects=True, vmem_limit_bytes=56 * 1024 * 1024
        ),
        name="ranker_step",
    )(
        tile_rows,
        tile_cols,
        tile_live,
        features,
        tile_vals,
        w_msg,
        w_self,
        w_dec,
        w_head.reshape(1, dec),
        sample_pairs.T,
        targets.reshape(per_device, tile),
    )
    big = [jax.ShapeDtypeStruct(out.shape, F32) for out in outs[:4]]
    grad_input, grad_msg, grad_self, grad_dec, grad_head, objective = pl.pallas_call(
        hand_out,
        out_shape=(*big, jax.ShapeDtypeStruct((1, dec), F32), jax.ShapeDtypeStruct((1, 1), F32)),
        in_specs=[in_vmem] * 5,
        out_specs=(in_vmem,) * 6,
        compiler_params=pltpu.CompilerParams(vmem_limit_bytes=16 * 1024 * 1024),
        name="hand_out",
    )(*outs)
    return objective.reshape(1), grad_msg, grad_self, grad_dec, grad_head.reshape(dec), grad_input


def solution(mesh):
    in_specs = (
        P(("grp", "blk"), None),
        P(("grp", "blk")),
        P(("grp", "blk")),
        P(("grp", "blk")),
        P(("grp", "blk"), None, None),
        P(),
        P(),
        P(),
        P(),
        P(("grp", "blk"), None),
        P(("grp", "blk")),
    )
    out_specs = (
        P("grp"),
        P("grp", "blk", None),
        P("grp", "blk", None),
        P(("grp", "blk"), None),
        P("grp"),
        P(("grp", "blk"), None),
    )
    return jax.shard_map(shards, mesh=mesh, in_specs=in_specs, out_specs=out_specs, check_vma=False)
```

```python
import functools

import jax
import jax.numpy as jnp
from jax import lax
from jax.experimental import pallas as pl
from jax.experimental.pallas import tpu as pltpu
from jax.sharding import PartitionSpec as P

LAYERS = 3
HB = 2
TABLE_ROWS = 8
PAIR_CHUNK = 512
norm_eps = 1e-05

F32 = jnp.float32
BF16 = jnp.bfloat16


def dot_nn(a, b):
    return jnp.dot(a, b, preferred_element_type=F32)


def dot_nt(a, b):
    return lax.dot_general(a, b, (((1,), (1,)), ((), ())), preferred_element_type=F32)


def dot_tn(a, b):
    return lax.dot_general(a, b, (((0,), (0,)), ((), ())), preferred_element_type=F32)


def two_parts(values):
    upper = values.astype(BF16)
    return upper, (values - upper.astype(F32)).astype(BF16)


def step(
    n,
    tile_rows,
    tile_cols,
    tile_live,
    feat,
    vals_in,
    w_msg_in,
    w_self_in,
    w_dec_in,
    w_head,
    pairs,
    targets,
    grad_input,
    grad_msg,
    grad_self,
    grad_dec,
    small_out,
    vals,
    w_msg,
    w_self,
    w_dec,
    band,
    rim,
    halo,
    hidden,
    message,
    update,
    slope,
    inverse,
    pooled,
    activ,
    head_slope,
    d_pooled,
    carried,
    d_update,
    d_mixed,
    d_message,
    d_halo,
    table,
    d_part,
    d_recv,
    small,
    small_recv,
    dec_part,
    dec_recv,
    w_part,
    w_near,
    w_sum,
    w_recv,
    target_table,
    load_sem,
    pair_send,
    pair_recv,
    chip_send,
    chip_recv,
    near_send,
    near_recv,
    all_send,
    all_recv,
):
    row_count, width = feat.shape
    slots, tile, _ = vals.shape
    per_device = row_count // tile
    half = HB * tile
    rows_out = width // n
    pair_total = pairs.shape[1]
    block_total = per_device * n
    me = lax.axis_index("blk")
    core, chip, chips = lax.rem(me, 2), me // 2, n // 2
    order = (1 - core, core)

    def each_peer(act):
        def visit(k, carry):
            act(lax.rem(me + k, n))
            return carry

        lax.fori_loop(1, n, visit, 0)

    loads = [
        pltpu.make_async_copy(there, here, load_sem.at[i])
        for i, (there, here) in enumerate(
            ((vals_in, vals), (w_msg_in, w_msg), (w_self_in, w_self), (w_dec_in, w_dec))
        )
    ]
    for load in loads:
        load.start()
    filler = jnp.zeros((TABLE_ROWS - per_device, tile), F32)
    target_table[me] = jnp.concatenate([targets[...], filler], axis=0)
    barrier = pltpu.get_barrier_semaphore()
    each_peer(
        lambda peer: pl.semaphore_signal(
            barrier, inc=1, device_id={"blk": peer}, device_id_type=pl.DeviceIdType.MESH
        )
    )
    pl.semaphore_wait(barrier, n - 1)

    def near(source, target, kind, side):
        return pltpu.make_async_remote_copy(
            src_ref=source,
            dst_ref=target,
            send_sem=near_send.at[kind, side],
            recv_sem=near_recv.at[kind, 1 - side],
            device_id={"blk": lax.rem(me + n - 1 + 2 * side, n)},
            device_id_type=pl.DeviceIdType.MESH,
        )

    def near_arrival(target, kind, side):
        return pltpu.make_async_remote_copy(
            src_ref=target,
            dst_ref=target,
            send_sem=near_send.at[kind, side],
            recv_sem=near_recv.at[kind, side],
            device_id={"blk": lax.rem(me + n - 1, n)},
            device_id_type=pl.DeviceIdType.MESH,
        )

    def far(source, target, kind, peer, slot):
        return pltpu.make_async_remote_copy(
            src_ref=source,
            dst_ref=target,
            send_sem=all_send.at[kind, peer],
            recv_sem=all_recv.at[kind, slot],
            device_id={"blk": peer},
            device_id_type=pl.DeviceIdType.MESH,
        )

    def scatter(parts, received, kind):
        each_peer(lambda peer: far(parts.at[peer], received.at[me], kind, peer, me).start())

    def arrived(received, kind):
        each_peer(lambda peer: far(received.at[peer], received.at[peer], kind, peer, peer).wait_recv())

    def all_sent(part, kind):
        each_peer(lambda peer: far(part, part, kind, peer, me).wait_send())

    middle = pl.ds(half, row_count)

    def half_rows(side):
        return pl.ds(pl.multiple_of(side * (row_count - half), tile), half)

    def rim_cols(side):
        return pl.ds(pl.multiple_of(side * (row_count + half), tile), half)

    sent = []

    def send_halves(source, target, kind, side):
        copy = near(source.at[half_rows(side)], target.at[1 - side], kind, side)
        copy.start()
        sent.append(copy)

    for side in order[::-1]:
        send_halves(feat, halo.at[0], 0, side)

    each_peer(lambda peer: far(target_table.at[me], target_table.at[me], 4, peer, me).start())
    loads[0].wait()

    for r in range(per_device):
        for e in range(HB, per_device + HB):
            if not r <= e <= r + 2 * HB:
                band[pl.ds(r * tile, tile), pl.ds(e * tile, tile)] = jnp.zeros((tile, tile), BF16)
    for r in range(1, HB):
        for e in range(r):
            band[pl.ds(r * tile, tile), pl.ds(e * tile, tile)] = jnp.zeros((tile, tile), BF16)
            far_row, far_col = per_device - 1 - r, per_device + 2 * HB - 1 - e
            band[pl.ds(far_row * tile, tile), pl.ds(far_col * tile, tile)] = jnp.zeros((tile, tile), BF16)
    live = tile_live[0]

    def fill_row(r, carry):
        totals = [jnp.zeros((tile, tile), F32)] * (2 * HB + 1)
        for t in range(slots):
            shift = lax.rem(tile_cols[t] - tile_rows[t] + HB + block_total, block_total)
            here = jnp.logical_and(tile_rows[t] - me * per_device == r, t < live)
            values = vals[t].astype(F32)
            for d in range(2 * HB + 1):
                chosen = jnp.where(jnp.logical_and(here, shift == d), 1.0, 0.0).astype(F32)
                totals[d] = totals[d] + values * chosen
        at_row = pl.ds(pl.multiple_of(r * tile, tile), tile)
        for d in range(2 * HB + 1):
            at_col = pl.ds(pl.multiple_of((r + d) * tile, tile), tile)
            band[at_row, at_col] = totals[d].astype(BF16)
        return carry

    lax.fori_loop(0, per_device, fill_row, 0)
    for side in order[::-1]:
        copy = near(band.at[half_rows(side), rim_cols(side)], rim.at[1 - side], 6, side)
        copy.start()
        sent.append(copy)

    for load in loads[1:]:
        load.wait()
    for layer in range(LAYERS):
        source = feat if layer == 0 else hidden.at[layer - 1]
        carried[...] = dot_nn(band[:, middle], source[...])
        for side in order:
            rows = half_rows(side)
            near_arrival(halo.at[layer, side], layer, side).wait_recv()
            term = dot_nn(band[rows, rim_cols(side)], halo[layer, side])
            msg = (carried[rows] + term).astype(BF16)
            message[layer, rows] = msg
            old = source[rows]
            mixed = dot_nn(msg, w_msg[layer]) + dot_nn(old, w_self[layer])
            squash = jax.nn.sigmoid(mixed)
            upd = old.astype(F32) + mixed * squash
            inv = lax.rsqrt(jnp.sum(upd * upd, axis=-1, keepdims=True) * (1.0 / width) + norm_eps)
            hidden[layer, rows] = (upd * inv).astype(BF16)
            if layer + 1 < LAYERS:
                send_halves(hidden.at[layer], halo.at[layer + 1], layer + 1, side)
            update[layer, rows] = upd
            inverse[layer, rows] = inv
            slope[layer, rows] = squash * (1.0 + mixed * (1.0 - squash))

    pool = hidden[0].astype(F32)
    for layer in range(1, LAYERS):
        pool = pool + hidden[layer].astype(F32)
    pooled[...] = pool.astype(BF16)
    pre_head = dot_nn(pooled[...], w_dec[...])
    squash = jax.nn.sigmoid(pre_head)
    act = pre_head * squash
    activ[...] = act
    head_slope[...] = squash * (1.0 + pre_head * (1.0 - squash))
    head_row = w_head[...]
    own_rows = []
    for b in range(per_device):
        block = act[b * tile : (b + 1) * tile] * head_row
        own_rows.append(jnp.sum(jnp.transpose(block), axis=0, keepdims=True))
    own_rows.append(filler)
    table[me] = jnp.concatenate(own_rows, axis=0)
    each_peer(lambda peer: far(table.at[me], table.at[me], 0, peer, me).start())

    arrived(target_table, 4)
    table_rows = n * TABLE_ROWS
    chunk = min(PAIR_CHUNK, pair_total)
    upper, lower = two_parts(target_table[...].reshape(table_rows, tile))
    lanes = lax.broadcasted_iota(jnp.int32, (tile, 2 * chunk), 0)
    at_row = lax.broadcasted_iota(jnp.int32, (table_rows, 2 * chunk), 0)
    prepared = []
    for c in range(pair_total // chunk):
        span = slice(c * chunk, (c + 1) * chunk)
        index = jnp.concatenate([pairs[0:1, span], pairs[1:2, span]], axis=1)
        low_hot = jnp.where(lanes == (index & (tile - 1)), 1.0, 0.0).astype(BF16)
        block_id = index >> 7
        place = lax.shift_right_logical(block_id, 2) * TABLE_ROWS + (block_id & 3)
        found = dot_nn(upper, low_hot) + dot_nn(lower, low_hot)
        target = jnp.sum(jnp.where(at_row == place, found, 0.0), axis=0, keepdims=True)
        wanted = jax.nn.sigmoid(target[:, :chunk] - target[:, chunk:])
        prepared.append((low_hot, place, wanted))
    arrived(table, 0)

    upper, lower = two_parts(table[...].reshape(table_rows, tile))
    total_d = jnp.zeros((table_rows, tile), F32)
    loss = jnp.zeros((1, chunk), F32)
    for low_hot, place, wanted in prepared:
        found = dot_nn(upper, low_hot) + dot_nn(lower, low_hot)
        in_scores = at_row == place
        score = jnp.sum(jnp.where(in_scores, found, 0.0), axis=0, keepdims=True)
        margin = score[:, :chunk] - score[:, chunk:]
        softplus = jnp.maximum(margin, 0.0) + jnp.log1p(jnp.exp(-jnp.abs(margin)))
        loss = loss + (softplus - wanted * margin)
        d_margin = (jax.nn.sigmoid(margin) - wanted) * (1.0 / pair_total)
        d_both = jnp.concatenate([d_margin, -d_margin], axis=1)
        d_upper = d_both.astype(BF16).astype(F32)
        d_lower = d_both - d_upper
        total_d = total_d + dot_nt(jnp.where(in_scores, d_upper, 0.0).astype(BF16), low_hot)
        total_d = total_d + dot_nt(jnp.where(in_scores, d_lower, 0.0).astype(BF16), low_hot)
    d_part[...] = total_d.reshape(n, TABLE_ROWS, tile)
    scatter(d_part, d_recv, 1)
    d_recv[me] = d_part[me]
    loss_here = jnp.sum(loss, axis=1, keepdims=True) * (1.0 / pair_total)
    arrived(d_recv, 1)
    d_scores = jnp.sum(d_recv[...], axis=0)

    head_sum = jnp.zeros((1, tile), F32)
    for b in range(per_device):
        rows = pl.ds(b * tile, tile)
        column = jnp.transpose(jnp.broadcast_to(d_scores[b : b + 1, :], (tile, tile)))
        head_sum = head_sum + jnp.sum(activ[rows] * column, axis=0, keepdims=True)
        d_pre = (column * head_row * head_slope[rows]).astype(BF16)
        d_mixed[rows, pl.ds(0, tile)] = d_pre
    d_pre = d_mixed[:, pl.ds(0, tile)]
    pooled_grad = dot_nt(d_pre, w_dec[...])
    d_pooled[...] = pooled_grad
    carried[...] = pooled_grad

    def weight_sends(layer):
        msg_term = dot_tn(message[layer], d_mixed[...])
        own = feat[...] if layer == 0 else hidden[layer - 1]
        self_term = dot_tn(own, d_mixed[...])
        for j in range(n):
            cut = slice(j * rows_out, (j + 1) * rows_out)
            w_part[layer, j % 2, j // 2, 0] = msg_term[cut].astype(w_part.dtype)
            w_part[layer, j % 2, j // 2, 1] = self_term[cut].astype(w_part.dtype)
        beside(layer).start()

    def beside(layer):
        return pltpu.make_async_remote_copy(
            src_ref=w_part.at[layer, 1 - core],
            dst_ref=w_near.at[layer],
            send_sem=pair_send.at[layer],
            recv_sem=pair_recv.at[layer],
            device_id={"blk": me + 1 - 2 * core},
            device_id_type=pl.DeviceIdType.MESH,
        )

    def chip_copy(layer, other, slot):
        return pltpu.make_async_remote_copy(
            src_ref=w_sum.at[layer, other],
            dst_ref=w_recv.at[layer, slot],
            send_sem=chip_send.at[layer, other],
            recv_sem=chip_recv.at[layer, slot],
            device_id={"blk": other * 2 + core},
            device_id_type=pl.DeviceIdType.MESH,
        )

    def each_chip(act):
        def visit(k, carry):
            act(lax.rem(chip + k, chips))
            return carry

        lax.fori_loop(1, chips, visit, 0)

    def chip_sends(layer):
        beside(layer).wait_recv()
        both = w_part[layer, core].astype(F32) + w_near[layer].astype(F32)
        w_sum[layer] = both.astype(w_sum.dtype)
        each_chip(lambda other: chip_copy(layer, other, chip).start())
        w_recv[layer, chip] = w_sum[layer, chip]

    def weight_sums(layer):
        each_chip(lambda other: chip_copy(layer, other, other).wait_recv())
        total = jnp.sum(w_recv[layer].astype(F32), axis=0)
        grad_msg[layer] = total[0]
        grad_self[layer] = total[1]

    for layer in reversed(range(LAYERS)):
        if layer == LAYERS - 1:
            dec_term = dot_tn(pooled[...], d_pre)
        for side in order[::-1]:
            rows = half_rows(side)
            inv = inverse[layer, rows]
            upd = update[layer, rows]
            carry = carried[rows]
            along = jnp.sum(carry * upd, axis=-1, keepdims=True) * (1.0 / width)
            d_upd = inv * carry - upd * (inv * inv * inv * along)
            d_update[rows] = d_upd
            mix = (d_upd * slope[layer, rows]).astype(BF16)
            d_mixed[rows] = mix
            d_message[layer, rows] = dot_nt(mix, w_msg[layer]).astype(BF16)
            send_halves(d_message.at[layer], d_halo.at[layer], 3 + layer, side)
        if layer == LAYERS - 1:
            for j in range(n):
                dec_part[j] = dec_term[j * rows_out : (j + 1) * rows_out].astype(dec_part.dtype)
            scatter(dec_part, dec_recv, 2)
            dec_recv[me] = dec_part[me]
            below = jnp.zeros((TABLE_ROWS - 2, tile), F32)
            loss_row = jnp.broadcast_to(loss_here, (1, tile))
            small[...] = jnp.concatenate([head_sum, loss_row, below], axis=0)
            each_peer(lambda peer: far(small, small_recv.at[me], 3, peer, me).start())
            small_recv[me] = small[...]
        weight_sends(layer)
        total = d_update[...] + dot_nt(d_mixed[...], w_self[layer])
        total = total + dot_tn(band[:, middle], d_message[layer])
        chip_sends(layer)
        if layer > 0:
            total = total + d_pooled[...]
        else:
            arrived(dec_recv, 2)
            grad_dec[...] = jnp.sum(dec_recv[...].astype(F32), axis=0)
            arrived(small_recv, 3)
            small_out[...] = jnp.sum(small_recv[...], axis=0)
            weight_sums(2)
        d_update[...] = total
        result = carried if layer > 0 else grad_input
        for side in order:
            rows = half_rows(side)
            if layer == LAYERS - 1:
                near_arrival(rim.at[side], 6, side).wait_recv()
            near_arrival(d_halo.at[layer, side], 3 + layer, side).wait_recv()
            term = dot_tn(rim[side], d_halo[layer, side])
            result[rows] = d_update[rows] + term
    weight_sums(1)
    weight_sums(0)
    for copy in sent:
        copy.wait_send()
    all_sent(table.at[me], 0)
    all_sent(d_part.at[me], 1)
    all_sent(dec_part.at[me], 2)
    all_sent(small, 3)
    all_sent(target_table.at[me], 4)
    for layer in range(LAYERS):
        beside(layer).wait_send()
        each_chip(lambda other: chip_copy(layer, other, chip).wait_send())


def hand_out(*refs):
    sources, targets, (small, sems) = refs[:5], refs[5:11], refs[11:]
    copies = [
        pltpu.make_async_copy(source, target, sems.at[i])
        for i, (source, target) in enumerate(zip(sources, (*targets[:4], small)))
    ]
    for copy in copies:
        copy.start()
    for copy in copies:
        copy.wait()
    targets[4][...] = small[0:1]
    targets[5][...] = small[1:2, 0:1]


def shards(
    features,
    tile_rows,
    tile_cols,
    tile_live,
    tile_vals,
    w_msg,
    w_self,
    w_dec,
    w_head,
    sample_pairs,
    targets,
):
    n = lax.axis_size("blk")
    row_count, width = features.shape
    tile = tile_vals.shape[1]
    per_device = row_count // tile
    dec = w_dec.shape[1]
    half = HB * tile
    rows_out = width // n
    wire = BF16 if rows_out % 16 == 0 else F32
    in_smem = pl.BlockSpec(memory_space=pltpu.SMEM)
    in_vmem = pl.BlockSpec(memory_space=pltpu.VMEM)
    outs = pl.pallas_call(
        functools.partial(step, n),
        out_shape=(
            jax.ShapeDtypeStruct((row_count, width), F32),
            jax.ShapeDtypeStruct((LAYERS, rows_out, width), F32),
            jax.ShapeDtypeStruct((LAYERS, rows_out, width), F32),
            jax.ShapeDtypeStruct((rows_out, dec), F32),
            jax.ShapeDtypeStruct((TABLE_ROWS, tile), F32),
        ),
        in_specs=[in_smem] * 3 + [in_vmem] + [pl.BlockSpec(memory_space=pl.ANY)] * 4 + [in_vmem] * 3,
        out_specs=(in_vmem,) * 5,
        scratch_shapes=[
            pltpu.VMEM(tile_vals.shape, BF16),
            pltpu.VMEM(w_msg.shape, BF16),
            pltpu.VMEM(w_self.shape, BF16),
            pltpu.VMEM(w_dec.shape, BF16),
            pltpu.VMEM((row_count, row_count + 2 * half), BF16),
            pltpu.VMEM((2, half, half), BF16),
            pltpu.VMEM((LAYERS, 2, half, width), BF16),
            pltpu.VMEM((LAYERS, row_count, width), BF16),
            pltpu.VMEM((LAYERS, row_count, width), BF16),
            pltpu.VMEM((LAYERS, row_count, width), F32),
            pltpu.VMEM((LAYERS, row_count, width), F32),
            pltpu.VMEM((LAYERS, row_count, 1), F32),
            pltpu.VMEM((row_count, width), BF16),
            pltpu.VMEM((row_count, dec), F32),
            pltpu.VMEM((row_count, dec), F32),
            pltpu.VMEM((row_count, width), F32),
            pltpu.VMEM((row_count, width), F32),
            pltpu.VMEM((row_count, width), F32),
            pltpu.VMEM((row_count, width), BF16),
            pltpu.VMEM((LAYERS, row_count, width), BF16),
            pltpu.VMEM((LAYERS, 2, half, width), BF16),
            pltpu.VMEM((n, TABLE_ROWS, tile), F32),
            pltpu.VMEM((n, TABLE_ROWS, tile), F32),
            pltpu.VMEM((n, TABLE_ROWS, tile), F32),
            pltpu.VMEM((TABLE_ROWS, tile), F32),
            pltpu.VMEM((n, TABLE_ROWS, tile), F32),
            pltpu.VMEM((n, rows_out, dec), wire),
            pltpu.VMEM((n, rows_out, dec), wire),
            pltpu.VMEM((LAYERS, 2, n // 2, 2, rows_out, width), wire),
            pltpu.VMEM((LAYERS, n // 2, 2, rows_out, width), wire),
            pltpu.VMEM((LAYERS, n // 2, 2, rows_out, width), wire),
            pltpu.VMEM((LAYERS, n // 2, 2, rows_out, width), wire),
            pltpu.VMEM((n, TABLE_ROWS, tile), F32),
            pltpu.SemaphoreType.DMA((4,)),
            pltpu.SemaphoreType.DMA((LAYERS,)),
            pltpu.SemaphoreType.DMA((LAYERS,)),
            pltpu.SemaphoreType.DMA((LAYERS, n // 2)),
            pltpu.SemaphoreType.DMA((LAYERS, n // 2)),
            pltpu.SemaphoreType.DMA((7, 2)),
            pltpu.SemaphoreType.DMA((7, 2)),
            pltpu.SemaphoreType.DMA((5, n)),
            pltpu.SemaphoreType.DMA((5, n)),
        ],
        compiler_params=pltpu.CompilerParams(
            collective_id=0, has_side_effects=True, vmem_limit_bytes=56 * 1024 * 1024
        ),
        name="ranker_step",
    )(
        tile_rows,
        tile_cols,
        tile_live,
        features,
        tile_vals,
        w_msg,
        w_self,
        w_dec,
        w_head.reshape(1, dec),
        sample_pairs.T,
        targets.reshape(per_device, tile),
    )
    big = [jax.ShapeDtypeStruct(out.shape, F32) for out in outs[:4]]
    grad_input, grad_msg, grad_self, grad_dec, grad_head, objective = pl.pallas_call(
        hand_out,
        out_shape=(*big, jax.ShapeDtypeStruct((1, dec), F32), jax.ShapeDtypeStruct((1, 1), F32)),
        in_specs=[pl.BlockSpec(memory_space=pl.ANY)] * 5,
        out_specs=(in_vmem,) * 6,
        scratch_shapes=[
            pltpu.VMEM((TABLE_ROWS, tile), F32),
            pltpu.SemaphoreType.DMA((5,)),
        ],
        compiler_params=pltpu.CompilerParams(vmem_limit_bytes=60 * 1024 * 1024),
        name="hand_out",
    )(*outs)
    return objective.reshape(1), grad_msg, grad_self, grad_dec, grad_head.reshape(dec), grad_input


def solution(mesh):
    in_specs = (
        P(("grp", "blk"), None),
        P(("grp", "blk")),
        P(("grp", "blk")),
        P(("grp", "blk")),
        P(("grp", "blk"), None, None),
        P(),
        P(),
        P(),
        P(),
        P(("grp", "blk"), None),
        P(("grp", "blk")),
    )
    out_specs = (
        P("grp"),
        P("grp", "blk", None),
        P("grp", "blk", None),
        P(("grp", "blk"), None),
        P("grp"),
        P(("grp", "blk"), None),
    )
    return jax.shard_map(shards, mesh=mesh, in_specs=in_specs, out_specs=out_specs, check_vma=False)
```

```python
import functools

import jax
import jax.numpy as jnp
from jax import lax
from jax.experimental import pallas as pl
from jax.experimental.pallas import tpu as pltpu
from jax.sharding import PartitionSpec as P

LAYERS = 3
HB = 2
TABLE_ROWS = 8
PAIR_CHUNK = 512
norm_eps = 1e-05

F32 = jnp.float32
BF16 = jnp.bfloat16


def dot_nn(a, b):
    return jnp.dot(a, b, preferred_element_type=F32)


def dot_nt(a, b):
    return lax.dot_general(a, b, (((1,), (1,)), ((), ())), preferred_element_type=F32)


def dot_tn(a, b):
    return lax.dot_general(a, b, (((0,), (0,)), ((), ())), preferred_element_type=F32)


def two_parts(values):
    upper = values.astype(BF16)
    return upper, (values - upper.astype(F32)).astype(BF16)


def step(
    n,
    tile_rows,
    tile_cols,
    tile_live,
    feat,
    vals_in,
    w_msg_in,
    w_self_in,
    w_dec_in,
    w_head,
    pairs,
    targets,
    grad_input,
    grad_msg,
    grad_self,
    grad_dec,
    small_out,
    vals,
    w_msg,
    w_self,
    w_dec,
    band,
    rim,
    halo,
    hidden,
    message,
    update,
    slope,
    inverse,
    pooled,
    activ,
    head_slope,
    d_pooled,
    carried,
    d_update,
    d_mixed,
    d_message,
    d_halo,
    table,
    d_part,
    d_recv,
    small,
    small_recv,
    dec_part,
    dec_recv,
    w_part,
    w_near,
    w_sum,
    w_recv,
    target_table,
    load_sem,
    pair_send,
    pair_recv,
    chip_send,
    chip_recv,
    near_send,
    near_recv,
    all_send,
    all_recv,
):
    row_count, width = feat.shape
    slots, tile, _ = vals.shape
    per_device = row_count // tile
    half = HB * tile
    rows_out = width // n
    pair_total = pairs.shape[1]
    block_total = per_device * n
    me = lax.axis_index("blk")
    core, chip, chips = lax.rem(me, 2), me // 2, n // 2
    order = (1 - core, core)

    def each_peer(act):
        def visit(k, carry):
            act(lax.rem(me + k, n))
            return carry

        lax.fori_loop(1, n, visit, 0)

    loads = [
        pltpu.make_async_copy(there, here, load_sem.at[i])
        for i, (there, here) in enumerate(
            ((vals_in, vals), (w_msg_in, w_msg), (w_self_in, w_self), (w_dec_in, w_dec))
        )
    ]
    for load in loads:
        load.start()
    filler = jnp.zeros((TABLE_ROWS - per_device, tile), F32)
    target_table[me] = jnp.concatenate([targets[...], filler], axis=0)
    barrier = pltpu.get_barrier_semaphore()
    each_peer(
        lambda peer: pl.semaphore_signal(
            barrier, inc=1, device_id={"blk": peer}, device_id_type=pl.DeviceIdType.MESH
        )
    )
    pl.semaphore_wait(barrier, n - 1)

    def near(source, target, kind, side):
        return pltpu.make_async_remote_copy(
            src_ref=source,
            dst_ref=target,
            send_sem=near_send.at[kind, side],
            recv_sem=near_recv.at[kind, 1 - side],
            device_id={"blk": lax.rem(me + n - 1 + 2 * side, n)},
            device_id_type=pl.DeviceIdType.MESH,
        )

    def near_arrival(target, kind, side):
        return pltpu.make_async_remote_copy(
            src_ref=target,
            dst_ref=target,
            send_sem=near_send.at[kind, side],
            recv_sem=near_recv.at[kind, side],
            device_id={"blk": lax.rem(me + n - 1, n)},
            device_id_type=pl.DeviceIdType.MESH,
        )

    def far(source, target, kind, peer, slot):
        return pltpu.make_async_remote_copy(
            src_ref=source,
            dst_ref=target,
            send_sem=all_send.at[kind, peer],
            recv_sem=all_recv.at[kind, slot],
            device_id={"blk": peer},
            device_id_type=pl.DeviceIdType.MESH,
        )

    def scatter(parts, received, kind):
        each_peer(lambda peer: far(parts.at[peer], received.at[me], kind, peer, me).start())

    def arrived(received, kind):
        each_peer(lambda peer: far(received.at[peer], received.at[peer], kind, peer, peer).wait_recv())

    def all_sent(part, kind):
        each_peer(lambda peer: far(part, part, kind, peer, me).wait_send())

    middle = pl.ds(half, row_count)

    def half_rows(side):
        return pl.ds(pl.multiple_of(side * (row_count - half), tile), half)

    def rim_cols(side):
        return pl.ds(pl.multiple_of(side * (row_count + half), tile), half)

    sent = []

    def send_halves(source, target, kind, side):
        copy = near(source.at[half_rows(side)], target.at[1 - side], kind, side)
        copy.start()
        sent.append(copy)

    for side in order[::-1]:
        send_halves(feat, halo.at[0], 0, side)

    each_peer(lambda peer: far(target_table.at[me], target_table.at[me], 4, peer, me).start())
    loads[0].wait()

    for r in range(per_device):
        for e in range(HB, per_device + HB):
            if not r <= e <= r + 2 * HB:
                band[pl.ds(r * tile, tile), pl.ds(e * tile, tile)] = jnp.zeros((tile, tile), BF16)
    for r in range(1, HB):
        for e in range(r):
            band[pl.ds(r * tile, tile), pl.ds(e * tile, tile)] = jnp.zeros((tile, tile), BF16)
            far_row, far_col = per_device - 1 - r, per_device + 2 * HB - 1 - e
            band[pl.ds(far_row * tile, tile), pl.ds(far_col * tile, tile)] = jnp.zeros((tile, tile), BF16)
    live = tile_live[0]

    def fill_row(r, carry):
        totals = [jnp.zeros((tile, tile), F32)] * (2 * HB + 1)
        for t in range(slots):
            shift = lax.rem(tile_cols[t] - tile_rows[t] + HB + block_total, block_total)
            here = jnp.logical_and(tile_rows[t] - me * per_device == r, t < live)
            values = vals[t].astype(F32)
            for d in range(2 * HB + 1):
                chosen = jnp.where(jnp.logical_and(here, shift == d), 1.0, 0.0).astype(F32)
                totals[d] = totals[d] + values * chosen
        at_row = pl.ds(pl.multiple_of(r * tile, tile), tile)
        for d in range(2 * HB + 1):
            at_col = pl.ds(pl.multiple_of((r + d) * tile, tile), tile)
            band[at_row, at_col] = totals[d].astype(BF16)
        return carry

    lax.fori_loop(0, per_device, fill_row, 0)
    for side in order[::-1]:
        copy = near(band.at[half_rows(side), rim_cols(side)], rim.at[1 - side], 6, side)
        copy.start()
        sent.append(copy)

    for load in loads[1:]:
        load.wait()
    for layer in range(LAYERS):
        source = feat if layer == 0 else hidden.at[layer - 1]
        carried[...] = dot_nn(band[:, middle], source[...])
        for side in order:
            rows = half_rows(side)
            near_arrival(halo.at[layer, side], layer, side).wait_recv()
            term = dot_nn(band[rows, rim_cols(side)], halo[layer, side])
            msg = (carried[rows] + term).astype(BF16)
            message[layer, rows] = msg
            old = source[rows]
            mixed = dot_nn(msg, w_msg[layer]) + dot_nn(old, w_self[layer])
            squash = jax.nn.sigmoid(mixed)
            upd = old.astype(F32) + mixed * squash
            inv = lax.rsqrt(jnp.sum(upd * upd, axis=-1, keepdims=True) * (1.0 / width) + norm_eps)
            hidden[layer, rows] = (upd * inv).astype(BF16)
            if layer + 1 < LAYERS:
                send_halves(hidden.at[layer], halo.at[layer + 1], layer + 1, side)
            update[layer, rows] = upd
            inverse[layer, rows] = inv
            slope[layer, rows] = squash * (1.0 + mixed * (1.0 - squash))

    pool = hidden[0].astype(F32)
    for layer in range(1, LAYERS):
        pool = pool + hidden[layer].astype(F32)
    pooled[...] = pool.astype(BF16)
    pre_head = dot_nn(pooled[...], w_dec[...])
    squash = jax.nn.sigmoid(pre_head)
    act = pre_head * squash
    activ[...] = act
    head_slope[...] = squash * (1.0 + pre_head * (1.0 - squash))
    head_row = w_head[...]
    own_rows = []
    for b in range(per_device):
        block = act[b * tile : (b + 1) * tile] * head_row
        own_rows.append(jnp.sum(jnp.transpose(block), axis=0, keepdims=True))
    own_rows.append(filler)
    table[me] = jnp.concatenate(own_rows, axis=0)
    each_peer(lambda peer: far(table.at[me], table.at[me], 0, peer, me).start())

    arrived(target_table, 4)
    table_rows = n * TABLE_ROWS
    chunk = min(PAIR_CHUNK, pair_total)
    upper, lower = two_parts(target_table[...].reshape(table_rows, tile))
    lanes = lax.broadcasted_iota(jnp.int32, (tile, 2 * chunk), 0)
    at_row = lax.broadcasted_iota(jnp.int32, (table_rows, 2 * chunk), 0)
    prepared = []
    for c in range(pair_total // chunk):
        span = slice(c * chunk, (c + 1) * chunk)
        index = jnp.concatenate([pairs[0:1, span], pairs[1:2, span]], axis=1)
        low_hot = jnp.where(lanes == (index & (tile - 1)), 1.0, 0.0).astype(BF16)
        block_id = index >> 7
        place = lax.shift_right_logical(block_id, 2) * TABLE_ROWS + (block_id & 3)
        found = dot_nn(upper, low_hot) + dot_nn(lower, low_hot)
        target = jnp.sum(jnp.where(at_row == place, found, 0.0), axis=0, keepdims=True)
        wanted = jax.nn.sigmoid(target[:, :chunk] - target[:, chunk:])
        prepared.append((low_hot, place, wanted))
    arrived(table, 0)

    upper, lower = two_parts(table[...].reshape(table_rows, tile))
    total_d = jnp.zeros((table_rows, tile), F32)
    loss = jnp.zeros((1, chunk), F32)
    for low_hot, place, wanted in prepared:
        found = dot_nn(upper, low_hot) + dot_nn(lower, low_hot)
        in_scores = at_row == place
        score = jnp.sum(jnp.where(in_scores, found, 0.0), axis=0, keepdims=True)
        margin = score[:, :chunk] - score[:, chunk:]
        softplus = jnp.maximum(margin, 0.0) + jnp.log1p(jnp.exp(-jnp.abs(margin)))
        loss = loss + (softplus - wanted * margin)
        d_margin = (jax.nn.sigmoid(margin) - wanted) * (1.0 / pair_total)
        d_both = jnp.concatenate([d_margin, -d_margin], axis=1)
        d_upper = d_both.astype(BF16).astype(F32)
        d_lower = d_both - d_upper
        total_d = total_d + dot_nt(jnp.where(in_scores, d_upper, 0.0).astype(BF16), low_hot)
        total_d = total_d + dot_nt(jnp.where(in_scores, d_lower, 0.0).astype(BF16), low_hot)
    d_part[...] = total_d.reshape(n, TABLE_ROWS, tile)
    scatter(d_part, d_recv, 1)
    d_recv[me] = d_part[me]
    loss_here = jnp.sum(loss, axis=1, keepdims=True) * (1.0 / pair_total)
    arrived(d_recv, 1)
    d_scores = jnp.sum(d_recv[...], axis=0)

    head_sum = jnp.zeros((1, tile), F32)
    for b in range(per_device):
        rows = pl.ds(b * tile, tile)
        column = jnp.transpose(jnp.broadcast_to(d_scores[b : b + 1, :], (tile, tile)))
        head_sum = head_sum + jnp.sum(activ[rows] * column, axis=0, keepdims=True)
        d_pre = (column * head_row * head_slope[rows]).astype(BF16)
        d_mixed[rows, pl.ds(0, tile)] = d_pre
    d_pre = d_mixed[:, pl.ds(0, tile)]
    pooled_grad = dot_nt(d_pre, w_dec[...])
    d_pooled[...] = pooled_grad
    carried[...] = pooled_grad

    def weight_sends(layer):
        msg_term = dot_tn(message[layer], d_mixed[...])
        own = feat[...] if layer == 0 else hidden[layer - 1]
        self_term = dot_tn(own, d_mixed[...])
        for j in range(n):
            cut = slice(j * rows_out, (j + 1) * rows_out)
            w_part[layer, j % 2, j // 2, 0] = msg_term[cut].astype(w_part.dtype)
            w_part[layer, j % 2, j // 2, 1] = self_term[cut].astype(w_part.dtype)
        beside(layer).start()

    def beside(layer):
        return pltpu.make_async_remote_copy(
            src_ref=w_part.at[layer, 1 - core],
            dst_ref=w_near.at[layer],
            send_sem=pair_send.at[layer],
            recv_sem=pair_recv.at[layer],
            device_id={"blk": me + 1 - 2 * core},
            device_id_type=pl.DeviceIdType.MESH,
        )

    def chip_copy(layer, other, slot):
        return pltpu.make_async_remote_copy(
            src_ref=w_sum.at[layer, other],
            dst_ref=w_recv.at[layer, slot],
            send_sem=chip_send.at[layer, other],
            recv_sem=chip_recv.at[layer, slot],
            device_id={"blk": other * 2 + core},
            device_id_type=pl.DeviceIdType.MESH,
        )

    def each_chip(act):
        def visit(k, carry):
            act(lax.rem(chip + k, chips))
            return carry

        lax.fori_loop(1, chips, visit, 0)

    def chip_sends(layer):
        beside(layer).wait_recv()
        both = w_part[layer, core].astype(F32) + w_near[layer].astype(F32)
        w_sum[layer] = both.astype(w_sum.dtype)
        each_chip(lambda other: chip_copy(layer, other, chip).start())
        w_recv[layer, chip] = w_sum[layer, chip]

    def weight_sums(layer):
        each_chip(lambda other: chip_copy(layer, other, other).wait_recv())
        total = jnp.sum(w_recv[layer].astype(F32), axis=0)
        grad_msg[layer] = total[0]
        grad_self[layer] = total[1]

    def open_half(layer, side):
        rows = half_rows(side)
        inv = inverse[layer, rows]
        upd = update[layer, rows]
        carry = carried[rows]
        along = jnp.sum(carry * upd, axis=-1, keepdims=True) * (1.0 / width)
        d_upd = inv * carry - upd * (inv * inv * inv * along)
        d_update[rows] = d_upd
        mix = (d_upd * slope[layer, rows]).astype(BF16)
        d_mixed[rows] = mix
        d_message[layer, rows] = dot_nt(mix, w_msg[layer]).astype(BF16)
        send_halves(d_message.at[layer], d_halo.at[layer], 3 + layer, side)

    for side in order[::-1]:
        open_half(LAYERS - 1, side)
    dec_term = dot_tn(pooled[...], d_pre)
    for layer in reversed(range(LAYERS)):
        if layer == LAYERS - 1:
            for j in range(n):
                dec_part[j] = dec_term[j * rows_out : (j + 1) * rows_out].astype(dec_part.dtype)
            scatter(dec_part, dec_recv, 2)
            dec_recv[me] = dec_part[me]
            below = jnp.zeros((TABLE_ROWS - 2, tile), F32)
            loss_row = jnp.broadcast_to(loss_here, (1, tile))
            small[...] = jnp.concatenate([head_sum, loss_row, below], axis=0)
            each_peer(lambda peer: far(small, small_recv.at[me], 3, peer, me).start())
            small_recv[me] = small[...]
        weight_sends(layer)
        total = d_update[...] + dot_nt(d_mixed[...], w_self[layer])
        total = total + dot_tn(band[:, middle], d_message[layer])
        chip_sends(layer)
        if layer > 0:
            total = total + d_pooled[...]
        else:
            arrived(dec_recv, 2)
            grad_dec[...] = jnp.sum(dec_recv[...].astype(F32), axis=0)
            arrived(small_recv, 3)
            small_out[...] = jnp.sum(small_recv[...], axis=0)
            weight_sums(2)
        d_update[...] = total
        result = carried if layer > 0 else grad_input
        for side in order:
            rows = half_rows(side)
            if layer == LAYERS - 1:
                near_arrival(rim.at[side], 6, side).wait_recv()
            near_arrival(d_halo.at[layer, side], 3 + layer, side).wait_recv()
            term = dot_tn(rim[side], d_halo[layer, side])
            result[rows] = d_update[rows] + term
            if layer > 0:
                open_half(layer - 1, side)
    weight_sums(1)
    weight_sums(0)
    for copy in sent:
        copy.wait_send()
    all_sent(table.at[me], 0)
    all_sent(d_part.at[me], 1)
    all_sent(dec_part.at[me], 2)
    all_sent(small, 3)
    all_sent(target_table.at[me], 4)
    for layer in range(LAYERS):
        beside(layer).wait_send()
        each_chip(lambda other: chip_copy(layer, other, chip).wait_send())


def hand_out(*refs):
    sources, targets, (small, sems) = refs[:5], refs[5:11], refs[11:]
    copies = [
        pltpu.make_async_copy(source, target, sems.at[i])
        for i, (source, target) in enumerate(zip(sources, (*targets[:4], small)))
    ]
    for copy in copies:
        copy.start()
    for copy in copies:
        copy.wait()
    targets[4][...] = small[0:1]
    targets[5][...] = small[1:2, 0:1]


def shards(
    features,
    tile_rows,
    tile_cols,
    tile_live,
    tile_vals,
    w_msg,
    w_self,
    w_dec,
    w_head,
    sample_pairs,
    targets,
):
    n = lax.axis_size("blk")
    row_count, width = features.shape
    tile = tile_vals.shape[1]
    per_device = row_count // tile
    dec = w_dec.shape[1]
    half = HB * tile
    rows_out = width // n
    wire = BF16 if rows_out % 16 == 0 else F32
    in_smem = pl.BlockSpec(memory_space=pltpu.SMEM)
    in_vmem = pl.BlockSpec(memory_space=pltpu.VMEM)
    outs = pl.pallas_call(
        functools.partial(step, n),
        out_shape=(
            jax.ShapeDtypeStruct((row_count, width), F32),
            jax.ShapeDtypeStruct((LAYERS, rows_out, width), F32),
            jax.ShapeDtypeStruct((LAYERS, rows_out, width), F32),
            jax.ShapeDtypeStruct((rows_out, dec), F32),
            jax.ShapeDtypeStruct((TABLE_ROWS, tile), F32),
        ),
        in_specs=[in_smem] * 3 + [in_vmem] + [pl.BlockSpec(memory_space=pl.ANY)] * 4 + [in_vmem] * 3,
        out_specs=(in_vmem,) * 5,
        scratch_shapes=[
            pltpu.VMEM(tile_vals.shape, BF16),
            pltpu.VMEM(w_msg.shape, BF16),
            pltpu.VMEM(w_self.shape, BF16),
            pltpu.VMEM(w_dec.shape, BF16),
            pltpu.VMEM((row_count, row_count + 2 * half), BF16),
            pltpu.VMEM((2, half, half), BF16),
            pltpu.VMEM((LAYERS, 2, half, width), BF16),
            pltpu.VMEM((LAYERS, row_count, width), BF16),
            pltpu.VMEM((LAYERS, row_count, width), BF16),
            pltpu.VMEM((LAYERS, row_count, width), F32),
            pltpu.VMEM((LAYERS, row_count, width), F32),
            pltpu.VMEM((LAYERS, row_count, 1), F32),
            pltpu.VMEM((row_count, width), BF16),
            pltpu.VMEM((row_count, dec), F32),
            pltpu.VMEM((row_count, dec), F32),
            pltpu.VMEM((row_count, width), F32),
            pltpu.VMEM((row_count, width), F32),
            pltpu.VMEM((row_count, width), F32),
            pltpu.VMEM((row_count, width), BF16),
            pltpu.VMEM((LAYERS, row_count, width), BF16),
            pltpu.VMEM((LAYERS, 2, half, width), BF16),
            pltpu.VMEM((n, TABLE_ROWS, tile), F32),
            pltpu.VMEM((n, TABLE_ROWS, tile), F32),
            pltpu.VMEM((n, TABLE_ROWS, tile), F32),
            pltpu.VMEM((TABLE_ROWS, tile), F32),
            pltpu.VMEM((n, TABLE_ROWS, tile), F32),
            pltpu.VMEM((n, rows_out, dec), wire),
            pltpu.VMEM((n, rows_out, dec), wire),
            pltpu.VMEM((LAYERS, 2, n // 2, 2, rows_out, width), wire),
            pltpu.VMEM((LAYERS, n // 2, 2, rows_out, width), wire),
            pltpu.VMEM((LAYERS, n // 2, 2, rows_out, width), wire),
            pltpu.VMEM((LAYERS, n // 2, 2, rows_out, width), wire),
            pltpu.VMEM((n, TABLE_ROWS, tile), F32),
            pltpu.SemaphoreType.DMA((4,)),
            pltpu.SemaphoreType.DMA((LAYERS,)),
            pltpu.SemaphoreType.DMA((LAYERS,)),
            pltpu.SemaphoreType.DMA((LAYERS, n // 2)),
            pltpu.SemaphoreType.DMA((LAYERS, n // 2)),
            pltpu.SemaphoreType.DMA((7, 2)),
            pltpu.SemaphoreType.DMA((7, 2)),
            pltpu.SemaphoreType.DMA((5, n)),
            pltpu.SemaphoreType.DMA((5, n)),
        ],
        compiler_params=pltpu.CompilerParams(
            collective_id=0, has_side_effects=True, vmem_limit_bytes=56 * 1024 * 1024
        ),
        name="ranker_step",
    )(
        tile_rows,
        tile_cols,
        tile_live,
        features,
        tile_vals,
        w_msg,
        w_self,
        w_dec,
        w_head.reshape(1, dec),
        sample_pairs.T,
        targets.reshape(per_device, tile),
    )
    big = [jax.ShapeDtypeStruct(out.shape, F32) for out in outs[:4]]
    grad_input, grad_msg, grad_self, grad_dec, grad_head, objective = pl.pallas_call(
        hand_out,
        out_shape=(*big, jax.ShapeDtypeStruct((1, dec), F32), jax.ShapeDtypeStruct((1, 1), F32)),
        in_specs=[pl.BlockSpec(memory_space=pl.ANY)] * 5,
        out_specs=(in_vmem,) * 6,
        scratch_shapes=[
            pltpu.VMEM((TABLE_ROWS, tile), F32),
            pltpu.SemaphoreType.DMA((5,)),
        ],
        compiler_params=pltpu.CompilerParams(vmem_limit_bytes=60 * 1024 * 1024),
        name="hand_out",
    )(*outs)
    return objective.reshape(1), grad_msg, grad_self, grad_dec, grad_head.reshape(dec), grad_input


def solution(mesh):
    in_specs = (
        P(("grp", "blk"), None),
        P(("grp", "blk")),
        P(("grp", "blk")),
        P(("grp", "blk")),
        P(("grp", "blk"), None, None),
        P(),
        P(),
        P(),
        P(),
        P(("grp", "blk"), None),
        P(("grp", "blk")),
    )
    out_specs = (
        P("grp"),
        P("grp", "blk", None),
        P("grp", "blk", None),
        P(("grp", "blk"), None),
        P("grp"),
        P(("grp", "blk"), None),
    )
    return jax.shard_map(shards, mesh=mesh, in_specs=in_specs, out_specs=out_specs, check_vma=False)
```
